256 devices in a mesh: pair: 8 (over z_lo, y), win: 32 (over z_hi, x, core).
Axes of the slice: x: 4, y: 4, z: 8 (z_hi: 4, z_lo: 2; z = z_hi * 2 + z_lo), core: 2. Of those that a mesh axis runs over, the one named last changes fastest.
Arguments:
- spectra: bfloat16 [2, 256, 256, 5120], P(None, 'win', None, 'pair'), may hold values from -3000 to 3000
- plan: int32 [7, 8], replicated, may hold values from 0 to 15, as said below
- round_index: int32 [1], replicated, may hold values from 0 to 6
Outputs:
- cross_spectra: bfloat16 [2, 4, 256, 640, 640], P(None, None, ('pair', 'win'))
The draws below stay inside these ranges and needn't reach their ends.
Inputs may be any that keep to these rules, and one draw needn't show every extreme that they name: `plan`: row r pairs the blocks: entry [r, q] mod 8 is the opponent of block q, the pairing is mutual, no block meets itself, over the 7 rows every block meets every other block once, and of each pair exactly one block has entry // 8 equal to 1.
All inputs are finite; a program needn't handle non-finite values.
Results may differ from the reference program's by a relative error of at most 0.0034.
Values may be sent and summed in bfloat16 or wider, within the bound.
No kernel may reach another device: no remote copies, remote signals or barrier semaphores. Data moves between devices by JAX's collectives and lax.ppermute only.
A program may use at most 64 MiB of HBM per device.

```python
import jax
import jax.numpy as jnp
from jax import lax

F = 256
B = 640
BLOCKS = 8
ROUNDS = 7
CHANNELS = 5120
WINDOWS = 256


def draw_spectra(key, part):
    key = jax.random.fold_in(key, 11)
    subkeys = jax.random.split(key, 5)
    noise_part = jnp.clip(jax.random.normal(subkeys[0], (2, WINDOWS, F, CHANNELS), jnp.float32), -5.0, 5.0)
    source = jnp.clip(jax.random.normal(subkeys[1], (2, WINDOWS, F, 1), jnp.float32), -5.0, 5.0)
    upper = 10.0
    channel_gain = jnp.clip(jax.random.normal(subkeys[2], (2, 1, 1, CHANNELS), jnp.float32), -5.0, 5.0)
    row_scale = jnp.exp(jax.random.uniform(subkeys[3], (1, WINDOWS, 1, CHANNELS), jnp.float32, 0.0, jnp.log(upper)))
    bin_scale = jnp.exp(jax.random.uniform(subkeys[4], (1, 1, F, 1), jnp.float32, jnp.log(0.3), jnp.log(3.0)))
    coherent_real = source[0] * channel_gain[0] - source[1] * channel_gain[1]
    coherent_imag = source[0] * channel_gain[1] + source[1] * channel_gain[0]
    coherent = 0.5 * jnp.stack([coherent_real, coherent_imag])
    return (row_scale * bin_scale * (coherent + noise_part)).astype(jnp.bfloat16)


def draw_plan(key, part):
    key = jax.random.fold_in(key, 23)
    label_key, round_key, side_key = jax.random.split(key, 3)
    modulus = BLOCKS - 1
    rounds = jnp.arange(ROUNDS, dtype=jnp.int32)[:, None]
    players = jnp.arange(BLOCKS, dtype=jnp.int32)[None, :]
    mirror = jnp.mod(2 * rounds - players, modulus)
    base = jnp.where(players == modulus, rounds, jnp.where(mirror == players, modulus, mirror)).astype(jnp.int32)
    labels = jax.random.permutation(label_key, BLOCKS).astype(jnp.int32)
    shuffle = jax.random.permutation(round_key, ROUNDS).astype(jnp.int32)
    base = jnp.take(base, shuffle, axis=0)
    renamed = jnp.take(labels, base)
    inverse = jnp.argsort(labels).astype(jnp.int32)
    opponents = jnp.take(renamed, inverse, axis=1).astype(jnp.int32)
    side_bits = jax.random.randint(side_key, (ROUNDS, BLOCKS), 0, 2).astype(jnp.int32)
    lower = jnp.minimum(players, opponents).astype(jnp.int32)
    lower_bit = jnp.take_along_axis(side_bits, lower, axis=1)
    home_flag = jnp.where(players < opponents, lower_bit, 1 - lower_bit).astype(jnp.int32)
    return (opponents + BLOCKS * home_flag).astype(jnp.int32)


def setup_inputs(seed: int = 0) -> dict:
    seeds = jax.random.split(jax.random.key(seed), 4)
    return {
        "spectra": draw_spectra(jax.random.fold_in(seeds[3], 71), 0),
        "plan": draw_plan(jax.random.fold_in(seeds[3], 71), 0),
        "round_index": jax.random.randint(seeds[2], (1,), 0, ROUNDS).astype(jnp.int32),
    }


EPS = 1e-06

def reference(spectra, plan, round_index):
    real_part = spectra[0].astype(jnp.float32)
    imag_part = spectra[1].astype(jnp.float32)
    energy = lax.optimization_barrier(jnp.mean(real_part * real_part + imag_part * imag_part, axis=1, keepdims=True))
    inverse = lax.rsqrt(energy + EPS)
    whitened = jnp.stack([real_part * inverse, imag_part * inverse]).astype(jnp.bfloat16)
    entries = jnp.take(plan, round_index, axis=0)[0].astype(jnp.int32)
    opponents = jnp.mod(entries, BLOCKS).astype(jnp.int32)
    home_flag = (entries // BLOCKS).astype(jnp.int32)
    ranking = jnp.argsort(jnp.where(home_flag == 1, 0, 1).astype(jnp.int32), stable=True)
    leaders = ranking[:BLOCKS // 2].astype(jnp.int32)
    highest = lax.Precision.HIGHEST

    def one_pair(leader):
        rival = jnp.take(opponents, leader).astype(jnp.int32)
        left_block = lax.dynamic_slice_in_dim(whitened, (leader * B).astype(jnp.int32), B, 3).astype(jnp.float32)
        right_block = lax.dynamic_slice_in_dim(whitened, (rival * B).astype(jnp.int32), B, 3).astype(jnp.float32)
        real_sum = jnp.einsum('wfi,wfj->fij', left_block[0], right_block[0], precision=highest)
        real_sum = real_sum + jnp.einsum('wfi,wfj->fij', left_block[1], right_block[1], precision=highest)
        imag_sum = jnp.einsum('wfi,wfj->fij', left_block[1], right_block[0], precision=highest)
        imag_sum = imag_sum - jnp.einsum('wfi,wfj->fij', left_block[0], right_block[1], precision=highest)
        return jnp.stack([real_sum, imag_sum]) / WINDOWS
    stacked = lax.map(one_pair, leaders)
    return jnp.swapaxes(stacked, 0, 1).astype(jnp.bfloat16)
```

```python
import jax
import jax.numpy as jnp
from jax import lax
from jax.experimental import pallas as pl
from jax.experimental.pallas import tpu as pltpu
from jax.sharding import PartitionSpec as P

EPS = 1e-06
LANES = 128


def whiten_kernel(x_ref, o_ref, scaled):
    _, windows, bins, _ = x_ref.shape
    for w in range(windows):
        real = x_ref[0, w].astype(jnp.float32)
        imag = x_ref[1, w].astype(jnp.float32)
        energy = jnp.mean(real * real + imag * imag, axis=0, keepdims=True)
        inverse = lax.rsqrt(energy + EPS)
        scaled[0, w * bins : (w + 1) * bins] = real * inverse
        scaled[1, w * bins : (w + 1) * bins] = imag * inverse
    for f in range(bins):
        rows = pl.ds(f, windows, stride=bins)
        o_ref[f] = jnp.concatenate([scaled[0, rows], scaled[1, rows]], axis=0).astype(o_ref.dtype)


def whiten(spectra):
    _, windows, bins, width = spectra.shape
    return pl.pallas_call(
        whiten_kernel,
        grid=(width // LANES,),
        in_specs=[pl.BlockSpec((2, windows, bins, LANES), lambda i: (0, 0, 0, i))],
        out_specs=pl.BlockSpec((bins, 2 * windows, LANES), lambda i: (0, 0, i)),
        out_shape=jax.ShapeDtypeStruct((bins, 2 * windows, width), jnp.bfloat16),
        scratch_shapes=[pltpu.VMEM((2, windows * bins, LANES), jnp.float32)],
        compiler_params=pltpu.CompilerParams(vmem_limit_bytes=48 * 1024 * 1024),
        name="whiten",
    )(spectra)


def leader_of(k, plan, round_index):
    row = round_index[0]
    seen = jnp.int32(0)
    leader = jnp.int32(0)
    for q in range(plan.shape[1]):
        home = plan[row, q] >> 3
        leader = leader + jnp.where(seen == k, home, 0) * q
        seen = seen + home
    return leader


def rival_of(k, plan, round_index):
    return plan[round_index[0], leader_of(k, plan, round_index)] & 7


def products_kernel(plan, round_index, lead_ref, trail_ref, o_ref):
    _, sources, parts, width = lead_ref.shape
    half = parts // 2
    rows = sources * parts
    lead = lead_ref[0].reshape(rows, width)
    trail = trail_ref[0]
    wide = trail.astype(jnp.float32)
    turned = jnp.concatenate([-wide[:, half:], wide[:, :half]], axis=1).astype(jnp.bfloat16)
    scale = 2.0 / rows
    for part, other in ((0, trail), (1, turned)):
        total = lax.dot_general(
            lead,
            other.reshape(rows, width),
            (((0,), (0,)), ((), ())),
            preferred_element_type=jnp.float32,
        )
        o_ref[part, 0] = (total * scale).astype(o_ref.dtype)


def products(arrived, plan, round_index):
    blocks, sources, parts, width = arrived.shape
    block = (1, sources, parts, width)
    return pl.pallas_call(
        products_kernel,
        grid_spec=pltpu.PrefetchScalarGridSpec(
            num_scalar_prefetch=2,
            grid=(blocks // 2,),
            in_specs=[
                pl.BlockSpec(block, lambda k, plan, ri: (leader_of(k, plan, ri), 0, 0, 0)),
                pl.BlockSpec(block, lambda k, plan, ri: (rival_of(k, plan, ri), 0, 0, 0)),
            ],
            out_specs=pl.BlockSpec((2, 1, width, width), lambda k, plan, ri: (0, k, 0, 0)),
        ),
        out_shape=jax.ShapeDtypeStruct((2, blocks // 2, width, width), jnp.bfloat16),
        compiler_params=pltpu.CompilerParams(vmem_limit_bytes=48 * 1024 * 1024),
        name="products",
    )(plan, round_index, arrived, arrived)


def body(spectra, plan, round_index):
    pair_count = lax.axis_size("pair")
    win_count = lax.axis_size("win")
    whitened = whiten(spectra)
    arrived = lax.all_to_all(whitened, ("pair", "win"), split_axis=0, concat_axis=0, tiled=True)
    arrived = arrived.reshape(pair_count, win_count, *arrived.shape[1:])
    return products(arrived, plan, round_index)[:, :, None]


def solution(mesh):
    placed = (P(None, "win", None, "pair"), P(), P())
    return jax.shard_map(
        body,
        mesh=mesh,
        in_specs=placed,
        out_specs=P(None, None, ("pair", "win"), None, None),
        check_vma=False,
    )
```

```python
import jax
import jax.numpy as jnp
from jax import lax
from jax.experimental import pallas as pl
from jax.experimental.pallas import tpu as pltpu
from jax.sharding import PartitionSpec as P

EPS = 1e-06
LANES = 128
ROWS = 32
GROUP = 16
VMEM_LIMIT = 24 * 1024 * 1024


def list_pairs(plan, round_index, pairs):
    blocks = plan.shape[1]
    entries = [plan[round_index[0], q] for q in range(blocks)]
    for k in range(blocks // 2):
        seen = jnp.int32(0)
        leader = jnp.int32(0)
        rival = jnp.int32(0)
        for q, entry in enumerate(entries):
            home = entry >> 3
            hit = jnp.where(seen == k, home, 0)
            leader = leader + hit * q
            rival = rival + hit * (entry & 7)
            seen = seen + home
        pairs[0, k] = leader
        pairs[1, k] = rival


def whiten_kernel(plan_hbm, round_hbm, x_hbm, o_ref, pairs, x_vmem, scale, plan, round_index, sems, small_sems):
    _, windows, bins, width = x_hbm.shape

    def copy(w):
        return pltpu.make_async_copy(x_hbm.at[:, w], x_vmem.at[:, w], sems.at[w])

    small = (
        pltpu.make_async_copy(plan_hbm, plan, small_sems.at[0]),
        pltpu.make_async_copy(round_hbm, round_index, small_sems.at[1]),
    )
    for c in small:
        c.start()
    for w in range(windows):
        copy(w).start()

    series = 2 * windows
    count = series * GROUP
    row = lax.broadcasted_iota(jnp.int32, (count, count), 0)
    column = lax.broadcasted_iota(jnp.int32, (count, count), 1)
    source = lax.rem(row, series) * GROUP + lax.div(row, series)
    swap = jnp.where(column == source, 1.0, 0.0).astype(jnp.bfloat16)

    for c in small:
        c.wait()
    list_pairs(plan, round_index, pairs)

    def one_window(w, carry):
        copy(w).wait()
        energies = []
        for lane in range(0, width, LANES):
            lanes = slice(lane, lane + LANES)
            totals = [jnp.zeros((8, LANES), jnp.float32) for _ in range(4)]
            for f in range(0, bins, ROWS):
                for part in range(2):
                    v = x_vmem[part, w, f : f + ROWS, lanes].astype(jnp.float32)
                    v = (v * v).reshape(ROWS // 8, 8, LANES)
                    for r in range(ROWS // 8):
                        totals[r % 4] = totals[r % 4] + v[r]
            total = (totals[0] + totals[1]) + (totals[2] + totals[3])
            energies.append(jnp.sum(total, axis=0, keepdims=True))
        energy = jnp.concatenate(energies, axis=1) * (1.0 / bins)
        scale[pl.ds(w, 1)] = lax.rsqrt(energy + EPS)
        return carry

    lax.fori_loop(0, windows, one_window, 0)
    inverse = scale[...]

    def one_group(g, carry):
        rows = pl.ds(pl.multiple_of(g * GROUP, GROUP), GROUP)
        moved = jnp.dot(swap, x_vmem[:, :, rows, :].reshape(count, width), preferred_element_type=jnp.float32)
        whitened = moved.reshape(2 * GROUP, windows, width) * inverse
        o_ref[rows] = whitened.astype(o_ref.dtype).reshape(GROUP, series, width)
        return carry

    lax.fori_loop(0, bins // GROUP, one_group, 0, unroll=True)


def whiten(spectra, plan, round_index):
    _, windows, bins, width = spectra.shape
    hbm = pl.BlockSpec(memory_space=pltpu.HBM)
    plan = pltpu.with_memory_space_constraint(plan, pltpu.HBM)
    spectra = pltpu.with_memory_space_constraint(spectra, pltpu.HBM)
    return pl.pallas_call(
        whiten_kernel,
        in_specs=[hbm, hbm, hbm],
        out_specs=[pl.BlockSpec(memory_space=pltpu.VMEM), pl.BlockSpec(memory_space=pltpu.SMEM)],
        out_shape=[
            jax.ShapeDtypeStruct((bins, 2 * windows, width), jnp.bfloat16),
            jax.ShapeDtypeStruct((2, plan.shape[1] // 2), jnp.int32),
        ],
        scratch_shapes=[
            pltpu.VMEM((2, windows, bins, width), jnp.bfloat16),
            pltpu.VMEM((windows, width), jnp.float32),
            pltpu.SMEM(plan.shape, jnp.int32),
            pltpu.SMEM(round_index.shape, jnp.int32),
            pltpu.SemaphoreType.DMA((windows,)),
            pltpu.SemaphoreType.DMA((2,)),
        ],
        compiler_params=pltpu.CompilerParams(vmem_limit_bytes=VMEM_LIMIT),
        name="whiten",
    )(plan, round_index, spectra)


def products_kernel(pairs, a_ref, o_hbm, held, out_sems):
    blocks, sources, parts, width = a_ref.shape
    half = parts // 2
    rows = sources * parts
    scale = 2.0 / rows

    def sent(k, slot):
        return pltpu.make_async_copy(held.at[slot], o_hbm.at[:, k], out_sems.at[slot])

    for k in range(blocks // 2):
        lead = a_ref[pairs[0, k]].reshape(rows, width)
        trail = a_ref[pairs[1, k]]
        wide = trail.astype(jnp.float32)
        turned = jnp.concatenate([-wide[:, half:], wide[:, :half]], axis=1).astype(jnp.bfloat16)
        slot = k % 2
        if k >= 2:
            sent(k - 2, slot).wait()
        for part, other in ((0, trail), (1, turned)):
            total = lax.dot_general(
                lead,
                other.reshape(rows, width),
                (((0,), (0,)), ((), ())),
                preferred_element_type=jnp.float32,
            )
            held[slot, part] = (total * scale).astype(held.dtype)
        sent(k, slot).start()
    for k in range(blocks // 2 - 2, blocks // 2):
        sent(k, k % 2).wait()


def products(arrived, pairs):
    blocks, sources, parts, width = arrived.shape
    return pl.pallas_call(
        products_kernel,
        in_specs=[
            pl.BlockSpec(memory_space=pltpu.SMEM),
            pl.BlockSpec(memory_space=pltpu.VMEM),
        ],
        out_specs=pl.BlockSpec(memory_space=pl.ANY),
        out_shape=jax.ShapeDtypeStruct((2, blocks // 2, width, width), jnp.bfloat16),
        scratch_shapes=[
            pltpu.VMEM((2, 2, width, width), jnp.bfloat16),
            pltpu.SemaphoreType.DMA((2,)),
        ],
        compiler_params=pltpu.CompilerParams(vmem_limit_bytes=VMEM_LIMIT),
        name="products",
    )(pairs, arrived)


def body(spectra, plan, round_index):
    pair_count = lax.axis_size("pair")
    win_count = lax.axis_size("win")
    whitened, pairs = whiten(spectra, plan, round_index)
    arrived = lax.all_to_all(whitened, ("pair", "win"), split_axis=0, concat_axis=0, tiled=True)
    arrived = arrived.reshape(pair_count, win_count, *arrived.shape[1:])
    return products(arrived, pairs)[:, :, None]


def solution(mesh):
    placed = (P(None, "win", None, "pair"), P(), P())
    return jax.shard_map(
        body,
        mesh=mesh,
        in_specs=placed,
        out_specs=P(None, None, ("pair", "win"), None, None),
        check_vma=False,
    )
```

```python
import jax
import jax.numpy as jnp
from jax import lax
from jax.experimental import pallas as pl
from jax.experimental.pallas import tpu as pltpu
from jax.sharding import PartitionSpec as P

EPS = 1e-06
LANES = 128
ROWS = 32
GROUP = 16
TILE = 256
VMEM_LIMIT = 24 * 1024 * 1024


def list_pairs(plan, round_index, pairs):
    blocks = plan.shape[1]
    entries = [plan[round_index[0], q] for q in range(blocks)]
    for k in range(blocks // 2):
        seen = jnp.int32(0)
        leader = jnp.int32(0)
        rival = jnp.int32(0)
        for q, entry in enumerate(entries):
            home = entry >> 3
            hit = jnp.where(seen == k, home, 0)
            leader = leader + hit * q
            rival = rival + hit * (entry & 7)
            seen = seen + home
        pairs[0, k] = leader
        pairs[1, k] = rival


def whiten_kernel(plan_hbm, round_hbm, x_hbm, o_ref, pairs, x_vmem, scale, plan, round_index, sems, small_sems):
    _, windows, bins, width = x_hbm.shape

    def copy(w):
        return pltpu.make_async_copy(x_hbm.at[:, w], x_vmem.at[:, w], sems.at[w])

    small = (
        pltpu.make_async_copy(plan_hbm, plan, small_sems.at[0]),
        pltpu.make_async_copy(round_hbm, round_index, small_sems.at[1]),
    )
    for c in small:
        c.start()
    for w in range(windows):
        copy(w).start()

    series = 2 * windows
    count = series * GROUP
    row = lax.broadcasted_iota(jnp.int32, (count, count), 0)
    column = lax.broadcasted_iota(jnp.int32, (count, count), 1)
    source = lax.rem(row, series) * GROUP + lax.div(row, series)
    swap = jnp.where(column == source, 1.0, 0.0).astype(jnp.bfloat16)

    for c in small:
        c.wait()
    list_pairs(plan, round_index, pairs)

    def one_window(w, carry):
        copy(w).wait()
        energies = []
        for lane in range(0, width, LANES):
            lanes = slice(lane, lane + LANES)
            totals = [jnp.zeros((8, LANES), jnp.float32) for _ in range(4)]
            for f in range(0, bins, ROWS):
                for part in range(2):
                    v = x_vmem[part, w, f : f + ROWS, lanes].astype(jnp.float32)
                    v = (v * v).reshape(ROWS // 8, 8, LANES)
                    for r in range(ROWS // 8):
                        totals[r % 4] = totals[r % 4] + v[r]
            total = (totals[0] + totals[1]) + (totals[2] + totals[3])
            energies.append(jnp.sum(total, axis=0, keepdims=True))
        energy = jnp.concatenate(energies, axis=1) * (1.0 / bins)
        scale[pl.ds(w, 1)] = lax.rsqrt(energy + EPS)
        return carry

    lax.fori_loop(0, windows, one_window, 0)
    inverse = scale[...]

    def one_group(g, carry):
        rows = pl.ds(pl.multiple_of(g * GROUP, GROUP), GROUP)
        moved = jnp.dot(swap, x_vmem[:, :, rows, :].reshape(count, width), preferred_element_type=jnp.float32)
        whitened = moved.reshape(2 * GROUP, windows, width) * inverse
        o_ref[rows] = whitened.astype(o_ref.dtype).reshape(GROUP, series, width)
        return carry

    lax.fori_loop(0, bins // GROUP, one_group, 0, unroll=True)


def whiten(spectra, plan, round_index):
    _, windows, bins, width = spectra.shape
    hbm = pl.BlockSpec(memory_space=pltpu.HBM)
    plan = pltpu.with_memory_space_constraint(plan, pltpu.HBM)
    spectra = pltpu.with_memory_space_constraint(spectra, pltpu.HBM)
    return pl.pallas_call(
        whiten_kernel,
        in_specs=[hbm, hbm, hbm],
        out_specs=[pl.BlockSpec(memory_space=pltpu.VMEM), pl.BlockSpec(memory_space=pltpu.SMEM)],
        out_shape=[
            jax.ShapeDtypeStruct((bins, 2 * windows, width), jnp.bfloat16),
            jax.ShapeDtypeStruct((2, plan.shape[1] // 2), jnp.int32),
        ],
        scratch_shapes=[
            pltpu.VMEM((2, windows, bins, width), jnp.bfloat16),
            pltpu.VMEM((windows, width), jnp.float32),
            pltpu.SMEM(plan.shape, jnp.int32),
            pltpu.SMEM(round_index.shape, jnp.int32),
            pltpu.SemaphoreType.DMA((windows,)),
            pltpu.SemaphoreType.DMA((2,)),
        ],
        compiler_params=pltpu.CompilerParams(vmem_limit_bytes=VMEM_LIMIT),
        name="whiten",
    )(plan, round_index, spectra)


def products_kernel(pairs, a_ref, o_hbm, held, sems):
    blocks, sources, parts, width = a_ref.shape
    half = parts // 2
    rows = sources * parts
    scale = 2.0 / rows

    def sent(k, part):
        return pltpu.make_async_copy(held.at[part, k], o_hbm.at[part, k], sems.at[part, k])

    for k in range(blocks // 2):
        lead = a_ref[pairs[0, k]].reshape(rows, width)
        trail = a_ref[pairs[1, k]]
        wide = trail.astype(jnp.float32)
        turned = jnp.concatenate([-wide[:, half:], wide[:, :half]], axis=1).astype(jnp.bfloat16)
        both = jnp.concatenate([trail.reshape(rows, width), turned.reshape(rows, width)], axis=1)
        for first in range(0, 2 * width, TILE):
            total = lax.dot_general(
                lead,
                both[:, first : first + TILE],
                (((0,), (0,)), ((), ())),
                preferred_element_type=jnp.float32,
            )
            result = (total * scale).astype(held.dtype)
            last = first + result.shape[1]
            cut = min(max(width - first, 0), result.shape[1])
            if cut:
                held[0, k, :, first : first + cut] = result[:, :cut]
            if cut < result.shape[1]:
                held[1, k, :, first + cut - width : last - width] = result[:, cut:]
            if first < width <= last:
                sent(k, 0).start()
        sent(k, 1).start()
    for k in range(blocks // 2):
        for part in range(2):
            sent(k, part).wait()


def products(arrived, pairs):
    blocks, sources, parts, width = arrived.shape
    return pl.pallas_call(
        products_kernel,
        in_specs=[
            pl.BlockSpec(memory_space=pltpu.SMEM),
            pl.BlockSpec(memory_space=pltpu.VMEM),
        ],
        out_specs=pl.BlockSpec(memory_space=pl.ANY),
        out_shape=jax.ShapeDtypeStruct((2, blocks // 2, width, width), jnp.bfloat16),
        scratch_shapes=[
            pltpu.VMEM((2, blocks // 2, width, width), jnp.bfloat16),
            pltpu.SemaphoreType.DMA((2, blocks // 2)),
        ],
        compiler_params=pltpu.CompilerParams(vmem_limit_bytes=VMEM_LIMIT),
        name="products",
    )(pairs, arrived)


def body(spectra, plan, round_index):
    pair_count = lax.axis_size("pair")
    win_count = lax.axis_size("win")
    whitened, pairs = whiten(spectra, plan, round_index)
    arrived = lax.all_to_all(whitened, ("pair", "win"), split_axis=0, concat_axis=0, tiled=True)
    arrived = arrived.reshape(pair_count, win_count, *arrived.shape[1:])
    return products(arrived, pairs)[:, :, None]


def solution(mesh):
    placed = (P(None, "win", None, "pair"), P(), P())
    return jax.shard_map(
        body,
        mesh=mesh,
        in_specs=placed,
        out_specs=P(None, None, ("pair", "win"), None, None),
        check_vma=False,
    )
```

```python
import jax
import jax.numpy as jnp
from jax import lax
from jax.experimental import pallas as pl
from jax.experimental.pallas import tpu as pltpu
from jax.sharding import PartitionSpec as P

EPS = 1e-06
LANES = 128
ROWS = 32
GROUP = 16
TILE = 256
JOIN = 2
Z, Y, X, C = 8, 4, 4, 2
VMEM_LIMIT = 24 * 1024 * 1024


def slot_of(owner):
    pair, win = divmod(owner, Z // 2 * X * C)
    z, y, x, c = 2 * (win // (X * C)) + pair // Y, pair % Y, (win // C) % X, win % C
    return ((c * X + x) * Y + y) * Z + z


def list_pairs(plan, round_index, pairs):
    blocks = plan.shape[1]
    entries = [plan[round_index[0], q] for q in range(blocks)]
    for k in range(blocks // 2):
        seen = jnp.int32(0)
        leader = jnp.int32(0)
        rival = jnp.int32(0)
        for q, entry in enumerate(entries):
            home = entry >> 3
            hit = jnp.where(seen == k, home, 0)
            leader = leader + hit * q
            rival = rival + hit * (entry & 7)
            seen = seen + home
        pairs[0, k] = leader
        pairs[1, k] = rival


def whiten_kernel(plan_hbm, round_hbm, x_hbm, o_ref, pairs, x_vmem, scale, plan, round_index, sems, small_sems):
    _, windows, bins, width = x_hbm.shape

    def copy(w):
        return pltpu.make_async_copy(x_hbm.at[:, w], x_vmem.at[:, w], sems.at[w])

    small = (
        pltpu.make_async_copy(plan_hbm, plan, small_sems.at[0]),
        pltpu.make_async_copy(round_hbm, round_index, small_sems.at[1]),
    )
    for c in small:
        c.start()
    for w in range(windows):
        copy(w).start()

    series = 2 * windows
    count = series * GROUP
    row = lax.broadcasted_iota(jnp.int32, (count, count), 0)
    column = lax.broadcasted_iota(jnp.int32, (count, count), 1)
    source = lax.rem(row, series) * GROUP + lax.div(row, series)
    swap = jnp.where(column == source, 1.0, 0.0).astype(jnp.bfloat16)

    for c in small:
        c.wait()
    list_pairs(plan, round_index, pairs)

    def one_window(w, carry):
        copy(w).wait()
        energies = []
        for lane in range(0, width, LANES):
            lanes = slice(lane, lane + LANES)
            totals = [jnp.zeros((8, LANES), jnp.float32) for _ in range(4)]
            for f in range(0, bins, ROWS):
                for part in range(2):
                    v = x_vmem[part, w, f : f + ROWS, lanes].astype(jnp.float32)
                    v = (v * v).reshape(ROWS // 8, 8, LANES)
                    for r in range(ROWS // 8):
                        totals[r % 4] = totals[r % 4] + v[r]
            total = (totals[0] + totals[1]) + (totals[2] + totals[3])
            energies.append(jnp.sum(total, axis=0, keepdims=True))
        energy = jnp.concatenate(energies, axis=1) * (1.0 / bins)
        scale[pl.ds(w, 1)] = lax.rsqrt(energy + EPS)
        return carry

    lax.fori_loop(0, windows, one_window, 0)
    inverse = scale[...]

    for first in range(0, bins, JOIN * GROUP):
        groups = range(first, first + JOIN * GROUP, GROUP)
        rows = [x_vmem[:, :, f : f + GROUP].reshape(count, width) for f in groups]
        moved = jnp.dot(swap, jnp.concatenate(rows, axis=1), preferred_element_type=jnp.float32)
        for j, f in enumerate(groups):
            group = moved[:, j * width : (j + 1) * width].reshape(2 * GROUP, windows, width) * inverse
            group = group.astype(o_ref.dtype).reshape(GROUP, series, width)
            for i in range(GROUP):
                o_ref[slot_of(f + i)] = group[i]


def whiten(spectra, plan, round_index):
    _, windows, bins, width = spectra.shape
    hbm = pl.BlockSpec(memory_space=pltpu.HBM)
    plan = pltpu.with_memory_space_constraint(plan, pltpu.HBM)
    spectra = pltpu.with_memory_space_constraint(spectra, pltpu.HBM)
    return pl.pallas_call(
        whiten_kernel,
        in_specs=[hbm, hbm, hbm],
        out_specs=[pl.BlockSpec(memory_space=pltpu.VMEM), pl.BlockSpec(memory_space=pltpu.SMEM)],
        out_shape=[
            jax.ShapeDtypeStruct((bins, 2 * windows, width), jnp.bfloat16),
            jax.ShapeDtypeStruct((2, plan.shape[1] // 2), jnp.int32),
        ],
        scratch_shapes=[
            pltpu.VMEM((2, windows, bins, width), jnp.bfloat16),
            pltpu.VMEM((windows, width), jnp.float32),
            pltpu.SMEM(plan.shape, jnp.int32),
            pltpu.SMEM(round_index.shape, jnp.int32),
            pltpu.SemaphoreType.DMA((windows,)),
            pltpu.SemaphoreType.DMA((2,)),
        ],
        compiler_params=pltpu.CompilerParams(vmem_limit_bytes=VMEM_LIMIT),
        name="whiten",
    )(plan, round_index, spectra)


def products_kernel(pairs, a_ref, o_hbm, held, sems):
    pieces, ys, highs, lows, parts, width = a_ref.shape
    blocks = lows * ys
    half = parts // 2
    rows = pieces * highs * parts
    scale = 2.0 / rows

    def sent(k, part):
        return pltpu.make_async_copy(held.at[part, k], o_hbm.at[part, k], sems.at[part, k])

    for k in range(blocks // 2):
        lead = a_ref[:, pairs[0, k] & (Y - 1), :, pairs[0, k] >> 2].reshape(rows, width)
        trail = a_ref[:, pairs[1, k] & (Y - 1), :, pairs[1, k] >> 2].reshape(pieces * highs, parts, width)
        wide = trail.astype(jnp.float32)
        turned = jnp.concatenate([-wide[:, half:], wide[:, :half]], axis=1).astype(jnp.bfloat16)
        both = jnp.concatenate([trail.reshape(rows, width), turned.reshape(rows, width)], axis=1)
        for first in range(0, 2 * width, TILE):
            total = lax.dot_general(
                lead,
                both[:, first : first + TILE],
                (((0,), (0,)), ((), ())),
                preferred_element_type=jnp.float32,
            )
            result = (total * scale).astype(held.dtype)
            last = first + result.shape[1]
            cut = min(max(width - first, 0), result.shape[1])
            if cut:
                held[0, k, :, first : first + cut] = result[:, :cut]
            if cut < result.shape[1]:
                held[1, k, :, first + cut - width : last - width] = result[:, cut:]
            if first < width <= last:
                sent(k, 0).start()
        sent(k, 1).start()
    for k in range(blocks // 2):
        for part in range(2):
            sent(k, part).wait()


def products(arrived, pairs):
    *_, width = arrived.shape
    blocks = 2 * Y
    return pl.pallas_call(
        products_kernel,
        in_specs=[
            pl.BlockSpec(memory_space=pltpu.SMEM),
            pl.BlockSpec(memory_space=pltpu.VMEM),
        ],
        out_specs=pl.BlockSpec(memory_space=pl.ANY),
        out_shape=jax.ShapeDtypeStruct((2, blocks // 2, width, width), jnp.bfloat16),
        scratch_shapes=[
            pltpu.VMEM((2, blocks // 2, width, width), jnp.bfloat16),
            pltpu.SemaphoreType.DMA((2, blocks // 2)),
        ],
        compiler_params=pltpu.CompilerParams(vmem_limit_bytes=VMEM_LIMIT),
        name="products",
    )(pairs, arrived)


def body(spectra, plan, round_index):
    pair_count = lax.axis_size("pair")
    win_count = lax.axis_size("win")
    whitened, pairs = whiten(spectra, plan, round_index)
    order = sorted(range(pair_count * win_count), key=slot_of)
    arrived = lax.all_to_all(
        whitened, ("pair", "win"), split_axis=0, concat_axis=0, tiled=True, axis_index_groups=[order]
    )
    arrived = arrived.reshape(C * X, Y, Z // 2, 2, *arrived.shape[1:])
    return products(arrived, pairs)[:, :, None]


def solution(mesh):
    placed = (P(None, "win", None, "pair"), P(), P())
    return jax.shard_map(
        body,
        mesh=mesh,
        in_specs=placed,
        out_specs=P(None, None, ("pair", "win"), None, None),
        check_vma=False,
    )
```

```python
import jax
import jax.numpy as jnp
from jax import lax
from jax.experimental import pallas as pl
from jax.experimental.pallas import tpu as pltpu
from jax.sharding import PartitionSpec as P

EPS = 1e-06
LANES = 128
ROWS = 32
GROUP = 16
TILE = 256
JOIN = 2
Z, Y, X, C = 8, 4, 4, 2
VMEM_LIMIT = 24 * 1024 * 1024


def slot_of(owner):
    pair, win = divmod(owner, Z // 2 * X * C)
    z, y, x, c = 2 * (win // (X * C)) + pair // Y, pair % Y, (win // C) % X, win % C
    return ((c * X + x) * Y + y) * Z + z


def list_pairs(plan, round_index, pairs):
    blocks = plan.shape[1]
    entries = [plan[round_index[0], q] for q in range(blocks)]
    for k in range(blocks // 2):
        seen = jnp.int32(0)
        leader = jnp.int32(0)
        rival = jnp.int32(0)
        for q, entry in enumerate(entries):
            home = entry >> 3
            hit = jnp.where(seen == k, home, 0)
            leader = leader + hit * q
            rival = rival + hit * (entry & 7)
            seen = seen + home
        pairs[0, k] = leader
        pairs[1, k] = rival


def whiten_kernel(
    plan_hbm, round_hbm, x_hbm, o_ref, pairs, x_vmem, early, scale, plan, round_index, sems, small_sems
):
    _, windows, bins, width = x_hbm.shape

    def copy(w):
        return pltpu.make_async_copy(x_hbm.at[:, w], x_vmem.at[:, w], sems.at[w])

    small = (
        pltpu.make_async_copy(plan_hbm, plan, small_sems.at[0]),
        pltpu.make_async_copy(round_hbm, round_index, small_sems.at[1]),
    )
    for c in small:
        c.start()
    for w in range(windows):
        copy(w).start()

    half = windows // 2
    series = 2 * half
    count = series * GROUP
    row = lax.broadcasted_iota(jnp.int32, (count, count), 0)
    column = lax.broadcasted_iota(jnp.int32, (count, count), 1)
    source = lax.rem(row, series) * GROUP + lax.div(row, series)
    swap = jnp.where(column == source, 1.0, 0.0).astype(jnp.bfloat16)

    for c in small:
        c.wait()
    list_pairs(plan, round_index, pairs)

    def one_window(w, carry):
        copy(w).wait()
        energies = []
        for lane in range(0, width, LANES):
            lanes = slice(lane, lane + LANES)
            totals = [jnp.zeros((8, LANES), jnp.float32) for _ in range(4)]
            for f in range(0, bins, ROWS):
                for part in range(2):
                    v = x_vmem[part, w, f : f + ROWS, lanes].astype(jnp.float32)
                    v = (v * v).reshape(ROWS // 8, 8, LANES)
                    for r in range(ROWS // 8):
                        totals[r % 4] = totals[r % 4] + v[r]
            total = (totals[0] + totals[1]) + (totals[2] + totals[3])
            energies.append(jnp.sum(total, axis=0, keepdims=True))
        energy = jnp.concatenate(energies, axis=1) * (1.0 / bins)
        inverse = lax.rsqrt(energy + EPS)
        side = w // half
        for part in range(2):
            scale[side, pl.ds(part * half + w - side * half, 1)] = inverse
        return carry

    for side in range(2):
        lax.fori_loop(side * half, (side + 1) * half, one_window, 0)
        inverse = scale[side]
        for first in range(0, bins, JOIN * GROUP):
            groups = range(first, first + JOIN * GROUP, GROUP)
            rows = [x_vmem[:, side * half : (side + 1) * half, f : f + GROUP].reshape(count, width) for f in groups]
            moved = jnp.dot(swap, jnp.concatenate(rows, axis=1), preferred_element_type=jnp.float32)
            for j, f in enumerate(groups):
                group = moved[:, j * width : (j + 1) * width].reshape(GROUP, series, width) * inverse
                if side == 0:
                    early[f : f + GROUP] = group
                    continue
                group = jnp.concatenate([early[f : f + GROUP], group], axis=1).astype(o_ref.dtype)
                for i in range(GROUP):
                    o_ref[slot_of(f + i)] = group[i]


def whiten(spectra, plan, round_index):
    _, windows, bins, width = spectra.shape
    hbm = pl.BlockSpec(memory_space=pltpu.HBM)
    plan = pltpu.with_memory_space_constraint(plan, pltpu.HBM)
    spectra = pltpu.with_memory_space_constraint(spectra, pltpu.HBM)
    return pl.pallas_call(
        whiten_kernel,
        in_specs=[hbm, hbm, hbm],
        out_specs=[pl.BlockSpec(memory_space=pltpu.VMEM), pl.BlockSpec(memory_space=pltpu.SMEM)],
        out_shape=[
            jax.ShapeDtypeStruct((bins, 2 * windows, width), jnp.bfloat16),
            jax.ShapeDtypeStruct((2, plan.shape[1] // 2), jnp.int32),
        ],
        scratch_shapes=[
            pltpu.VMEM((2, windows, bins, width), jnp.bfloat16),
            pltpu.VMEM((bins, windows, width), jnp.float32),
            pltpu.VMEM((2, windows, width), jnp.float32),
            pltpu.SMEM(plan.shape, jnp.int32),
            pltpu.SMEM(round_index.shape, jnp.int32),
            pltpu.SemaphoreType.DMA((windows,)),
            pltpu.SemaphoreType.DMA((2,)),
        ],
        compiler_params=pltpu.CompilerParams(vmem_limit_bytes=VMEM_LIMIT),
        name="whiten",
    )(plan, round_index, spectra)


def products_kernel(pairs, a_ref, o_hbm, held, sems):
    pieces, ys, highs, lows, parts, width = a_ref.shape
    blocks = lows * ys
    half = parts // 4
    rows = pieces * highs * parts
    scale = 2.0 / rows

    def sent(k, part):
        return pltpu.make_async_copy(held.at[part, k], o_hbm.at[part, k], sems.at[part, k])

    row = lax.broadcasted_iota(jnp.int32, (1, 2 * half, width), 1)
    sign = jnp.where(row < half, -1.0, 1.0)
    for k in range(blocks // 2):
        lead = a_ref[:, pairs[0, k] & (Y - 1), :, pairs[0, k] >> 2].reshape(rows, width)
        trail = a_ref[:, pairs[1, k] & (Y - 1), :, pairs[1, k] >> 2].reshape(pieces * highs, parts, width)
        wide = trail.astype(jnp.float32).reshape(rows // (2 * half), 2 * half, width)
        turned = (pltpu.roll(wide, half, axis=1) * sign).astype(jnp.bfloat16)
        both = jnp.concatenate([trail.reshape(rows, width), turned.reshape(rows, width)], axis=1)
        for first in range(0, 2 * width, TILE):
            total = lax.dot_general(
                lead,
                both[:, first : first + TILE],
                (((0,), (0,)), ((), ())),
                preferred_element_type=jnp.float32,
            )
            result = (total * scale).astype(held.dtype)
            last = first + result.shape[1]
            cut = min(max(width - first, 0), result.shape[1])
            if cut:
                held[0, k, :, first : first + cut] = result[:, :cut]
            if cut < result.shape[1]:
                held[1, k, :, first + cut - width : last - width] = result[:, cut:]
            if first < width <= last:
                sent(k, 0).start()
        sent(k, 1).start()
    for k in range(blocks // 2):
        for part in range(2):
            sent(k, part).wait()


def products(arrived, pairs):
    *_, width = arrived.shape
    blocks = 2 * Y
    return pl.pallas_call(
        products_kernel,
        in_specs=[
            pl.BlockSpec(memory_space=pltpu.SMEM),
            pl.BlockSpec(memory_space=pltpu.VMEM),
        ],
        out_specs=pl.BlockSpec(memory_space=pl.ANY),
        out_shape=jax.ShapeDtypeStruct((2, blocks // 2, width, width), jnp.bfloat16),
        scratch_shapes=[
            pltpu.VMEM((2, blocks // 2, width, width), jnp.bfloat16),
            pltpu.SemaphoreType.DMA((2, blocks // 2)),
        ],
        compiler_params=pltpu.CompilerParams(vmem_limit_bytes=VMEM_LIMIT),
        name="products",
    )(pairs, arrived)


def body(spectra, plan, round_index):
    pair_count = lax.axis_size("pair")
    win_count = lax.axis_size("win")
    whitened, pairs = whiten(spectra, plan, round_index)
    order = sorted(range(pair_count * win_count), key=slot_of)
    arrived = lax.all_to_all(
        whitened, ("pair", "win"), split_axis=0, concat_axis=0, tiled=True, axis_index_groups=[order]
    )
    arrived = arrived.reshape(C * X, Y, Z // 2, 2, *arrived.shape[1:])
    return products(arrived, pairs)[:, :, None]


def solution(mesh):
    placed = (P(None, "win", None, "pair"), P(), P())
    return jax.shard_map(
        body,
        mesh=mesh,
        in_specs=placed,
        out_specs=P(None, None, ("pair", "win"), None, None),
        check_vma=False,
    )
```

```python
import jax
import jax.numpy as jnp
from jax import lax
from jax.experimental import pallas as pl
from jax.experimental.pallas import tpu as pltpu
from jax.sharding import PartitionSpec as P

EPS = 1e-06
LANES = 128
ROWS = 32
GROUP = 16
TILE = 256
JOIN = 2
Z, Y, X, C = 8, 4, 4, 2
VMEM_LIMIT = 24 * 1024 * 1024


def slot_of(owner):
    pair, win = divmod(owner, Z // 2 * X * C)
    z, y, x, c = 2 * (win // (X * C)) + pair // Y, pair % Y, (win // C) % X, win % C
    return ((c * X + x) * Y + y) * Z + z


def list_pairs(plan, round_index, pairs):
    blocks = plan.shape[1]
    entries = [plan[round_index[0], q] for q in range(blocks)]
    for k in range(blocks // 2):
        seen = jnp.int32(0)
        leader = jnp.int32(0)
        rival = jnp.int32(0)
        for q, entry in enumerate(entries):
            home = entry >> 3
            hit = jnp.where(seen == k, home, 0)
            leader = leader + hit * q
            rival = rival + hit * (entry & 7)
            seen = seen + home
        pairs[0, k] = leader
        pairs[1, k] = rival


def whiten_kernel(plan_hbm, round_hbm, x_hbm, o_ref, pairs, x_vmem, scale, plan, round_index, sems, small_sems):
    _, windows, bins, width = x_hbm.shape

    def copy(w):
        return pltpu.make_async_copy(x_hbm.at[:, w], x_vmem.at[:, w], sems.at[w])

    small = (
        pltpu.make_async_copy(plan_hbm, plan, small_sems.at[0]),
        pltpu.make_async_copy(round_hbm, round_index, small_sems.at[1]),
    )
    for c in small:
        c.start()
    for w in range(windows):
        copy(w).start()

    series = 2 * windows
    count = series * GROUP
    row = lax.broadcasted_iota(jnp.int32, (count, count), 0)
    column = lax.broadcasted_iota(jnp.int32, (count, count), 1)
    source = lax.rem(row, series) * GROUP + lax.div(row, series)
    swap = jnp.where(column == source, 1.0, 0.0).astype(jnp.bfloat16)

    for c in small:
        c.wait()
    list_pairs(plan, round_index, pairs)

    def one_window(w, carry):
        copy(w).wait()
        energies = []
        for lane in range(0, width, LANES):
            lanes = slice(lane, lane + LANES)
            totals = [jnp.zeros((8, LANES), jnp.float32) for _ in range(4)]
            for f in range(0, bins, ROWS):
                for part in range(2):
                    v = x_vmem[part, w, f : f + ROWS, lanes].astype(jnp.float32)
                    v = (v * v).reshape(ROWS // 8, 8, LANES)
                    for r in range(ROWS // 8):
                        totals[r % 4] = totals[r % 4] + v[r]
            total = (totals[0] + totals[1]) + (totals[2] + totals[3])
            energies.append(jnp.sum(total, axis=0, keepdims=True))
        energy = jnp.concatenate(energies, axis=1) * (1.0 / bins)
        scale[pl.ds(w, 1)] = lax.rsqrt(energy + EPS)
        return carry

    lax.fori_loop(0, windows, one_window, 0)
    inverse = scale[...]

    for first in range(0, bins, JOIN * GROUP):
        groups = range(first, first + JOIN * GROUP, GROUP)
        rows = [x_vmem[:, :, f : f + GROUP].reshape(count, width) for f in groups]
        moved = jnp.dot(swap, jnp.concatenate(rows, axis=1), preferred_element_type=jnp.float32)
        for j, f in enumerate(groups):
            group = moved[:, j * width : (j + 1) * width].reshape(2 * GROUP, windows, width) * inverse
            group = group.astype(o_ref.dtype).reshape(GROUP, series, width)
            for i in range(GROUP):
                o_ref[slot_of(f + i)] = group[i]


def whiten(spectra, plan, round_index):
    _, windows, bins, width = spectra.shape
    hbm = pl.BlockSpec(memory_space=pltpu.HBM)
    plan = pltpu.with_memory_space_constraint(plan, pltpu.HBM)
    spectra = pltpu.with_memory_space_constraint(spectra, pltpu.HBM)
    return pl.pallas_call(
        whiten_kernel,
        in_specs=[hbm, hbm, hbm],
        out_specs=[pl.BlockSpec(memory_space=pltpu.VMEM), pl.BlockSpec(memory_space=pltpu.SMEM)],
        out_shape=[
            jax.ShapeDtypeStruct((bins, 2 * windows, width), jnp.bfloat16),
            jax.ShapeDtypeStruct((2, plan.shape[1] // 2), jnp.int32),
        ],
        scratch_shapes=[
            pltpu.VMEM((2, windows, bins, width), jnp.bfloat16),
            pltpu.VMEM((windows, width), jnp.float32),
            pltpu.SMEM(plan.shape, jnp.int32),
            pltpu.SMEM(round_index.shape, jnp.int32),
            pltpu.SemaphoreType.DMA((windows,)),
            pltpu.SemaphoreType.DMA((2,)),
        ],
        compiler_params=pltpu.CompilerParams(vmem_limit_bytes=VMEM_LIMIT),
        name="whiten",
    )(plan, round_index, spectra)


def products_kernel(pairs, a_ref, o_hbm, held, sems):
    pieces, ys, highs, lows, parts, width = a_ref.shape
    blocks = lows * ys
    half = parts // 2
    rows = pieces * highs * parts
    scale = 2.0 / rows

    def sent(k, part, top, bottom):
        some = pl.ds(top, bottom - top)
        return pltpu.make_async_copy(
            held.at[part, k, some], o_hbm.at[part, k, some], sems.at[part, k, int(top > 0)]
        )

    copies = []
    for k in range(blocks // 2):
        lead = a_ref[:, pairs[0, k] & (Y - 1), :, pairs[0, k] >> 2].reshape(rows, width)
        trail = a_ref[:, pairs[1, k] & (Y - 1), :, pairs[1, k] >> 2].reshape(pieces * highs, parts, width)
        wide = trail.astype(jnp.float32)
        turned = jnp.concatenate([-wide[:, half:], wide[:, :half]], axis=1).astype(jnp.bfloat16)
        both = jnp.concatenate([trail.reshape(rows, width), turned.reshape(rows, width)], axis=1)
        cuts = (0, width - TILE, width) if k == blocks // 2 - 1 else (0, width)
        for top, bottom in zip(cuts[:-1], cuts[1:]):
            for first in range(0, 2 * width, TILE):
                total = lax.dot_general(
                    lead[:, top:bottom],
                    both[:, first : first + TILE],
                    (((0,), (0,)), ((), ())),
                    preferred_element_type=jnp.float32,
                )
                result = (total * scale).astype(held.dtype)
                last = first + result.shape[1]
                cut = min(max(width - first, 0), result.shape[1])
                if cut:
                    held[0, k, top:bottom, first : first + cut] = result[:, :cut]
                if cut < result.shape[1]:
                    held[1, k, top:bottom, first + cut - width : last - width] = result[:, cut:]
                if first < width <= last:
                    copies.append(sent(k, 0, top, bottom))
                    copies[-1].start()
            copies.append(sent(k, 1, top, bottom))
            copies[-1].start()
    for c in copies:
        c.wait()


def products(arrived, pairs):
    *_, width = arrived.shape
    blocks = 2 * Y
    return pl.pallas_call(
        products_kernel,
        in_specs=[
            pl.BlockSpec(memory_space=pltpu.SMEM),
            pl.BlockSpec(memory_space=pltpu.VMEM),
        ],
        out_specs=pl.BlockSpec(memory_space=pl.ANY),
        out_shape=jax.ShapeDtypeStruct((2, blocks // 2, width, width), jnp.bfloat16),
        scratch_shapes=[
            pltpu.VMEM((2, blocks // 2, width, width), jnp.bfloat16),
            pltpu.SemaphoreType.DMA((2, blocks // 2, 2)),
        ],
        compiler_params=pltpu.CompilerParams(vmem_limit_bytes=VMEM_LIMIT),
        name="products",
    )(pairs, arrived)


def body(spectra, plan, round_index):
    pair_count = lax.axis_size("pair")
    win_count = lax.axis_size("win")
    whitened, pairs = whiten(spectra, plan, round_index)
    order = sorted(range(pair_count * win_count), key=slot_of)
    arrived = lax.all_to_all(
        whitened, ("pair", "win"), split_axis=0, concat_axis=0, tiled=True, axis_index_groups=[order]
    )
    arrived = arrived.reshape(C * X, Y, Z // 2, 2, *arrived.shape[1:])
    return products(arrived, pairs)[:, :, None]


def solution(mesh):
    placed = (P(None, "win", None, "pair"), P(), P())
    return jax.shard_map(
        body,
        mesh=mesh,
        in_specs=placed,
        out_specs=P(None, None, ("pair", "win"), None, None),
        check_vma=False,
    )
```

```python
import jax
import jax.numpy as jnp
from jax import lax
from jax.experimental import pallas as pl
from jax.experimental.pallas import tpu as pltpu
from jax.sharding import PartitionSpec as P

EPS = 1e-06
LANES = 128
ROWS = 32
GROUP = 16
TILE = 256
JOIN = 2
Z, Y, X, C = 8, 4, 4, 2
VMEM_LIMIT = 24 * 1024 * 1024


def slot_of(owner):
    pair, win = divmod(owner, Z // 2 * X * C)
    z, y, x, c = 2 * (win // (X * C)) + pair // Y, pair % Y, (win // C) % X, win % C
    return ((c * X + x) * Y + y) * Z + z


def list_pairs(plan, round_index, pairs):
    blocks = plan.shape[1]
    entries = [plan[round_index[0], q] for q in range(blocks)]
    for k in range(blocks // 2):
        seen = jnp.int32(0)
        leader = jnp.int32(0)
        rival = jnp.int32(0)
        for q, entry in enumerate(entries):
            home = entry >> 3
            hit = jnp.where(seen == k, home, 0)
            leader = leader + hit * q
            rival = rival + hit * (entry & 7)
            seen = seen + home
        pairs[0, k] = leader
        pairs[1, k] = rival


def whiten_kernel(
    plan_hbm, round_hbm, x_hbm, o_ref, pairs, x_vmem, early, scale, plan, round_index, sems, small_sems
):
    _, windows, bins, width = x_hbm.shape

    def copy(w):
        return pltpu.make_async_copy(x_hbm.at[:, w], x_vmem.at[:, w], sems.at[w])

    small = (
        pltpu.make_async_copy(plan_hbm, plan, small_sems.at[0]),
        pltpu.make_async_copy(round_hbm, round_index, small_sems.at[1]),
    )
    for c in small:
        c.start()
    for w in range(windows):
        copy(w).start()

    half = windows // 2
    series = 2 * half
    count = series * GROUP
    row = lax.broadcasted_iota(jnp.int32, (count, count), 0)
    column = lax.broadcasted_iota(jnp.int32, (count, count), 1)
    source = lax.rem(row, series) * GROUP + lax.div(row, series)
    swap = jnp.where(column == source, 1.0, 0.0).astype(jnp.bfloat16)

    for c in small:
        c.wait()
    list_pairs(plan, round_index, pairs)

    def one_window(w, carry):
        copy(w).wait()
        energies = []
        for lane in range(0, width, LANES):
            lanes = slice(lane, lane + LANES)
            totals = [jnp.zeros((8, LANES), jnp.float32) for _ in range(4)]
            for f in range(0, bins, ROWS):
                for part in range(2):
                    v = x_vmem[part, w, f : f + ROWS, lanes].astype(jnp.float32)
                    v = (v * v).reshape(ROWS // 8, 8, LANES)
                    for r in range(ROWS // 8):
                        totals[r % 4] = totals[r % 4] + v[r]
            total = (totals[0] + totals[1]) + (totals[2] + totals[3])
            energies.append(jnp.sum(total, axis=0, keepdims=True))
        energy = jnp.concatenate(energies, axis=1) * (1.0 / bins)
        inverse = lax.rsqrt(energy + EPS)
        side = w // half
        for part in range(2):
            scale[side, pl.ds(part * half + w - side * half, 1)] = inverse
        return carry

    for side in range(2):
        lax.fori_loop(side * half, (side + 1) * half, one_window, 0)
        inverse = scale[side]
        for first in range(0, bins, JOIN * GROUP):
            groups = range(first, first + JOIN * GROUP, GROUP)
            rows = [x_vmem[:, side * half : (side + 1) * half, f : f + GROUP].reshape(count, width) for f in groups]
            moved = jnp.dot(swap, jnp.concatenate(rows, axis=1), preferred_element_type=jnp.float32)
            for j, f in enumerate(groups):
                group = moved[:, j * width : (j + 1) * width].reshape(GROUP, series, width) * inverse
                if side == 0:
                    early[f : f + GROUP] = group
                    continue
                group = jnp.concatenate([early[f : f + GROUP], group], axis=1).astype(o_ref.dtype)
                for i in range(GROUP):
                    o_ref[slot_of(f + i)] = group[i]


def whiten(spectra, plan, round_index):
    _, windows, bins, width = spectra.shape
    hbm = pl.BlockSpec(memory_space=pltpu.HBM)
    plan = pltpu.with_memory_space_constraint(plan, pltpu.HBM)
    spectra = pltpu.with_memory_space_constraint(spectra, pltpu.HBM)
    return pl.pallas_call(
        whiten_kernel,
        in_specs=[hbm, hbm, hbm],
        out_specs=[pl.BlockSpec(memory_space=pltpu.VMEM), pl.BlockSpec(memory_space=pltpu.SMEM)],
        out_shape=[
            jax.ShapeDtypeStruct((bins, 2 * windows, width), jnp.bfloat16),
            jax.ShapeDtypeStruct((2, plan.shape[1] // 2), jnp.int32),
        ],
        scratch_shapes=[
            pltpu.VMEM((2, windows, bins, width), jnp.bfloat16),
            pltpu.VMEM((bins, windows, width), jnp.float32),
            pltpu.VMEM((2, windows, width), jnp.float32),
            pltpu.SMEM(plan.shape, jnp.int32),
            pltpu.SMEM(round_index.shape, jnp.int32),
            pltpu.SemaphoreType.DMA((windows,)),
            pltpu.SemaphoreType.DMA((2,)),
        ],
        compiler_params=pltpu.CompilerParams(vmem_limit_bytes=VMEM_LIMIT),
        name="whiten",
    )(plan, round_index, spectra)


def products_kernel(pairs, a_ref, o_hbm, held, sems):
    pieces, ys, highs, lows, parts, width = a_ref.shape
    blocks = lows * ys
    half = parts // 4
    rows = pieces * highs * parts
    scale = 2.0 / rows

    def sent(k, part, top, bottom):
        some = pl.ds(top, bottom - top)
        return pltpu.make_async_copy(
            held.at[part, k, some], o_hbm.at[part, k, some], sems.at[part, k, int(top > 0)]
        )

    copies = []
    row = lax.broadcasted_iota(jnp.int32, (1, 2 * half, width), 1)
    sign = jnp.where(row < half, -1.0, 1.0)
    for k in range(blocks // 2):
        lead = a_ref[:, pairs[0, k] & (Y - 1), :, pairs[0, k] >> 2].reshape(rows, width)
        trail = a_ref[:, pairs[1, k] & (Y - 1), :, pairs[1, k] >> 2].reshape(pieces * highs, parts, width)
        wide = trail.astype(jnp.float32).reshape(rows // (2 * half), 2 * half, width)
        turned = (pltpu.roll(wide, half, axis=1) * sign).astype(jnp.bfloat16)
        both = jnp.concatenate([trail.reshape(rows, width), turned.reshape(rows, width)], axis=1)
        cuts = (0, width - TILE, width) if k == blocks // 2 - 1 else (0, width)
        for top, bottom in zip(cuts[:-1], cuts[1:]):
            for first in range(0, 2 * width, TILE):
                total = lax.dot_general(
                    lead[:, top:bottom],
                    both[:, first : first + TILE],
                    (((0,), (0,)), ((), ())),
                    preferred_element_type=jnp.float32,
                )
                result = (total * scale).astype(held.dtype)
                last = first + result.shape[1]
                cut = min(max(width - first, 0), result.shape[1])
                if cut:
                    held[0, k, top:bottom, first : first + cut] = result[:, :cut]
                if cut < result.shape[1]:
                    held[1, k, top:bottom, first + cut - width : last - width] = result[:, cut:]
                if first < width <= last:
                    copies.append(sent(k, 0, top, bottom))
                    copies[-1].start()
            copies.append(sent(k, 1, top, bottom))
            copies[-1].start()
    for c in copies:
        c.wait()


def products(arrived, pairs):
    *_, width = arrived.shape
    blocks = 2 * Y
    return pl.pallas_call(
        products_kernel,
        in_specs=[
            pl.BlockSpec(memory_space=pltpu.SMEM),
            pl.BlockSpec(memory_space=pltpu.VMEM),
        ],
        out_specs=pl.BlockSpec(memory_space=pl.ANY),
        out_shape=jax.ShapeDtypeStruct((2, blocks // 2, width, width), jnp.bfloat16),
        scratch_shapes=[
            pltpu.VMEM((2, blocks // 2, width, width), jnp.bfloat16),
            pltpu.SemaphoreType.DMA((2, blocks // 2, 2)),
        ],
        compiler_params=pltpu.CompilerParams(vmem_limit_bytes=VMEM_LIMIT),
        name="products",
    )(pairs, arrived)


def body(spectra, plan, round_index):
    pair_count = lax.axis_size("pair")
    win_count = lax.axis_size("win")
    whitened, pairs = whiten(spectra, plan, round_index)
    order = sorted(range(pair_count * win_count), key=slot_of)
    arrived = lax.all_to_all(
        whitened, ("pair", "win"), split_axis=0, concat_axis=0, tiled=True, axis_index_groups=[order]
    )
    arrived = arrived.reshape(C * X, Y, Z // 2, 2, *arrived.shape[1:])
    return products(arrived, pairs)[:, :, None]


def solution(mesh):
    placed = (P(None, "win", None, "pair"), P(), P())
    return jax.shard_map(
        body,
        mesh=mesh,
        in_specs=placed,
        out_specs=P(None, None, ("pair", "win"), None, None),
        check_vma=False,
    )
```

```python
import jax
import jax.numpy as jnp
from jax import lax
from jax.experimental import pallas as pl
from jax.experimental.pallas import tpu as pltpu
from jax.sharding import PartitionSpec as P

EPS = 1e-06
LANES = 128
ROWS = 32
GROUP = 16
TILE = 256
JOIN = 4
Z, Y, X, C = 8, 4, 4, 2
VMEM_LIMIT = 24 * 1024 * 1024


def slot_of(owner):
    pair, win = divmod(owner, Z // 2 * X * C)
    z, y, x, c = 2 * (win // (X * C)) + pair // Y, pair % Y, (win // C) % X, win % C
    return ((c * X + x) * Y + y) * Z + z


def list_pairs(plan, round_index, pairs):
    blocks = plan.shape[1]
    entries = [plan[round_index[0], q] for q in range(blocks)]
    for k in range(blocks // 2):
        seen = jnp.int32(0)
        leader = jnp.int32(0)
        rival = jnp.int32(0)
        for q, entry in enumerate(entries):
            home = entry >> 3
            hit = jnp.where(seen == k, home, 0)
            leader = leader + hit * q
            rival = rival + hit * (entry & 7)
            seen = seen + home
        pairs[0, k] = leader
        pairs[1, k] = rival


def whiten_kernel(
    plan_hbm, round_hbm, x_hbm, o_ref, pairs, x_vmem, early, scale, plan, round_index, sems, small_sems
):
    _, windows, bins, width = x_hbm.shape

    def copy(w):
        return pltpu.make_async_copy(x_hbm.at[:, w], x_vmem.at[:, w], sems.at[w])

    small = (
        pltpu.make_async_copy(plan_hbm, plan, small_sems.at[0]),
        pltpu.make_async_copy(round_hbm, round_index, small_sems.at[1]),
    )
    for c in small:
        c.start()
    for w in range(windows):
        copy(w).start()

    half = windows // 2
    series = 2 * half
    count = series * GROUP
    row = lax.broadcasted_iota(jnp.int32, (count, count), 0)
    column = lax.broadcasted_iota(jnp.int32, (count, count), 1)
    source = lax.rem(row, series) * GROUP + lax.div(row, series)
    swap = jnp.where(column == source, 1.0, 0.0).astype(jnp.bfloat16)

    for c in small:
        c.wait()
    list_pairs(plan, round_index, pairs)

    def one_window(w, carry):
        copy(w).wait()
        energies = []
        for lane in range(0, width, LANES):
            lanes = slice(lane, lane + LANES)
            totals = [jnp.zeros((8, LANES), jnp.float32) for _ in range(4)]
            for f in range(0, bins, ROWS):
                for part in range(2):
                    v = x_vmem[part, w, f : f + ROWS, lanes].astype(jnp.float32)
                    v = (v * v).reshape(ROWS // 8, 8, LANES)
                    for r in range(ROWS // 8):
                        totals[r % 4] = totals[r % 4] + v[r]
            total = (totals[0] + totals[1]) + (totals[2] + totals[3])
            energies.append(jnp.sum(total, axis=0, keepdims=True))
        energy = jnp.concatenate(energies, axis=1) * (1.0 / bins)
        inverse = lax.rsqrt(energy + EPS)
        side = w // half
        for part in range(2):
            scale[side, pl.ds(part * half + w - side * half, 1)] = inverse
        return carry

    for side in range(2):
        lax.fori_loop(side * half, (side + 1) * half, one_window, 0)
        inverse = scale[side]
        for first in range(0, bins, JOIN * GROUP):
            groups = range(first, first + JOIN * GROUP, GROUP)
            rows = [x_vmem[:, side * half : (side + 1) * half, f : f + GROUP].reshape(count, width) for f in groups]
            moved = jnp.dot(swap, jnp.concatenate(rows, axis=1), preferred_element_type=jnp.float32)
            for j, f in enumerate(groups):
                group = moved[:, j * width : (j + 1) * width].reshape(GROUP, series, width) * inverse
                if side == 0:
                    early[f : f + GROUP] = group
                    continue
                group = jnp.concatenate([early[f : f + GROUP], group], axis=1).astype(o_ref.dtype)
                for i in range(GROUP):
                    o_ref[slot_of(f + i)] = group[i]


def whiten(spectra, plan, round_index):
    _, windows, bins, width = spectra.shape
    hbm = pl.BlockSpec(memory_space=pltpu.HBM)
    plan = pltpu.with_memory_space_constraint(plan, pltpu.HBM)
    spectra = pltpu.with_memory_space_constraint(spectra, pltpu.HBM)
    return pl.pallas_call(
        whiten_kernel,
        in_specs=[hbm, hbm, hbm],
        out_specs=[pl.BlockSpec(memory_space=pltpu.VMEM), pl.BlockSpec(memory_space=pltpu.SMEM)],
        out_shape=[
            jax.ShapeDtypeStruct((bins, 2 * windows, width), jnp.bfloat16),
            jax.ShapeDtypeStruct((2, plan.shape[1] // 2), jnp.int32),
        ],
        scratch_shapes=[
            pltpu.VMEM((2, windows, bins, width), jnp.bfloat16),
            pltpu.VMEM((bins, windows, width), jnp.float32),
            pltpu.VMEM((2, windows, width), jnp.float32),
            pltpu.SMEM(plan.shape, jnp.int32),
            pltpu.SMEM(round_index.shape, jnp.int32),
            pltpu.SemaphoreType.DMA((windows,)),
            pltpu.SemaphoreType.DMA((2,)),
        ],
        compiler_params=pltpu.CompilerParams(vmem_limit_bytes=VMEM_LIMIT),
        name="whiten",
    )(plan, round_index, spectra)


def products_kernel(pairs, a_ref, o_hbm, held, sems):
    pieces, ys, highs, lows, parts, width = a_ref.shape
    blocks = lows * ys
    half = parts // 4
    rows = pieces * highs * parts
    scale = 2.0 / rows

    def sent(k, part, top, bottom):
        some = pl.ds(top, bottom - top)
        return pltpu.make_async_copy(
            held.at[part, k, some], o_hbm.at[part, k, some], sems.at[part, k, int(top > 0)]
        )

    copies = []
    row = lax.broadcasted_iota(jnp.int32, (1, 2 * half, width), 1)
    sign = jnp.where(row < half, -1.0, 1.0)
    for k in range(blocks // 2):
        lead = a_ref[:, pairs[0, k] & (Y - 1), :, pairs[0, k] >> 2].reshape(rows, width)
        trail = a_ref[:, pairs[1, k] & (Y - 1), :, pairs[1, k] >> 2].reshape(pieces * highs, parts, width)
        wide = trail.astype(jnp.float32).reshape(rows // (2 * half), 2 * half, width)
        turned = (pltpu.roll(wide, half, axis=1) * sign).astype(jnp.bfloat16)
        both = jnp.concatenate([trail.reshape(rows, width), turned.reshape(rows, width)], axis=1)
        cuts = (0, width - TILE, width) if k == blocks // 2 - 1 else (0, width)
        for top, bottom in zip(cuts[:-1], cuts[1:]):
            for first in range(0, 2 * width, TILE):
                total = lax.dot_general(
                    lead[:, top:bottom],
                    both[:, first : first + TILE],
                    (((0,), (0,)), ((), ())),
                    preferred_element_type=jnp.float32,
                )
                result = (total * scale).astype(held.dtype)
                last = first + result.shape[1]
                cut = min(max(width - first, 0), result.shape[1])
                if cut:
                    held[0, k, top:bottom, first : first + cut] = result[:, :cut]
                if cut < result.shape[1]:
                    held[1, k, top:bottom, first + cut - width : last - width] = result[:, cut:]
                if first < width <= last:
                    copies.append(sent(k, 0, top, bottom))
                    copies[-1].start()
            copies.append(sent(k, 1, top, bottom))
            copies[-1].start()
    for c in copies:
        c.wait()


def products(arrived, pairs):
    *_, width = arrived.shape
    blocks = 2 * Y
    return pl.pallas_call(
        products_kernel,
        in_specs=[
            pl.BlockSpec(memory_space=pltpu.SMEM),
            pl.BlockSpec(memory_space=pltpu.VMEM),
        ],
        out_specs=pl.BlockSpec(memory_space=pl.ANY),
        out_shape=jax.ShapeDtypeStruct((2, blocks // 2, width, width), jnp.bfloat16),
        scratch_shapes=[
            pltpu.VMEM((2, blocks // 2, width, width), jnp.bfloat16),
            pltpu.SemaphoreType.DMA((2, blocks // 2, 2)),
        ],
        compiler_params=pltpu.CompilerParams(vmem_limit_bytes=VMEM_LIMIT),
        name="products",
    )(pairs, arrived)


def body(spectra, plan, round_index):
    pair_count = lax.axis_size("pair")
    win_count = lax.axis_size("win")
    whitened, pairs = whiten(spectra, plan, round_index)
    order = sorted(range(pair_count * win_count), key=slot_of)
    arrived = lax.all_to_all(
        whitened, ("pair", "win"), split_axis=0, concat_axis=0, tiled=True, axis_index_groups=[order]
    )
    arrived = arrived.reshape(C * X, Y, Z // 2, 2, *arrived.shape[1:])
    return products(arrived, pairs)[:, :, None]


def solution(mesh):
    placed = (P(None, "win", None, "pair"), P(), P())
    return jax.shard_map(
        body,
        mesh=mesh,
        in_specs=placed,
        out_specs=P(None, None, ("pair", "win"), None, None),
        check_vma=False,
    )
```
